256 devices in a mesh: wide: 128 (over x, z_lo, y, core), narrow: 2 (over z_hi).
Axes of the slice: x: 4, y: 4, z: 8 (z_hi: 2, z_lo: 4; z = z_hi * 4 + z_lo), core: 2. Of those that a mesh axis runs over, the one named last changes fastest.
Arguments:
- tokens: bfloat16 [131072, 2048], P(('wide', 'narrow')), may hold values from -16 to 16
- slot_param: bfloat16 [2048, 512], P(None, 'wide'), may hold values from -4 to 4
- w_in: bfloat16 [128, 2048, 2048], P('wide', None, 'narrow'), may hold values from -0.125 to 0.125
- w_out: bfloat16 [128, 2048, 2048], P('wide', 'narrow'), may hold values from -0.125 to 0.125
Outputs:
- mixed: bfloat16 [131072, 2048], P(('wide', 'narrow'))
The draws below stay inside these ranges and needn't reach their ends.
All inputs are finite; a program needn't handle non-finite values.
Results may differ from the reference program's by a relative error of at most 0.022.
Values may be sent and summed in bfloat16 or wider, within the bound.
No kernel may reach another device: no remote copies, remote signals or barrier semaphores. Data moves between devices by JAX's collectives and lax.ppermute only.
A program may use at most 64 MiB of HBM per device.

```python
import jax
import jax.numpy as jnp
from jax import lax

D = 2048
FF = 2048
SLOTS = 4
TOK_DEV = 512
EXPERTS = 128
SLOTS_ALL = 512
TOKENS = 131072


def slot_table(key):
    return jnp.clip(jax.random.normal(jax.random.fold_in(key, 11), (D, SLOTS_ALL), jnp.float32), -4.0, 4.0)


def draw_slot_param(key, part):
    return slot_table(key).astype(jnp.bfloat16)


def draw_tokens(key, part):
    key = jax.random.fold_in(key, 3)
    blocks = TOKENS // TOK_DEV
    base_draw = jnp.clip(jax.random.normal(key, (blocks, TOK_DEV, D), jnp.float32), -6.0, 6.0)
    return jnp.clip(base_draw.reshape(TOKENS, D), -16.0, 16.0).astype(jnp.bfloat16)


def block_levels(rng, shape, shards, smallest, top_value):
    def one(position, parts):
        steps = jax.random.uniform(jax.random.fold_in(jax.random.fold_in(rng, 6), position), (parts,), jnp.float32, smallest / len(shards), top_value / len(shards))
        return jnp.repeat(jnp.exp(steps), shape[position] // parts).reshape((-1,) + (1,) * (len(shape) - position - 1))

    loudness = one(*shards[0])
    for cut in shards[1:]:
        loudness = loudness * one(*cut)
    return loudness


def centred(rng, dims, deviation, bound, cuts=(), held_as=jnp.bfloat16):
    values = deviation * jax.random.normal(rng, dims, jnp.float32)
    if cuts:
        values = values * block_levels(rng, dims, cuts, -0.22, 0.18)
    return jnp.clip(values, -bound, bound).astype(held_as)


def setup_inputs(seed: int = 0) -> dict:
    key_list = jax.random.split(jax.random.key(seed), 5)
    return {
        "tokens": draw_tokens(jax.random.fold_in(key_list[4], 71), 0),
        "slot_param": draw_slot_param(jax.random.fold_in(key_list[4], 71), 0),
        "w_in": centred(key_list[2], (EXPERTS, D, FF), D ** -0.5, 0.125, ((0, 128), (2, 2))),
        "w_out": centred(key_list[3], (EXPERTS, FF, D), FF ** -0.5, 0.125, ((0, 128), (1, 2))),
    }


logit_scale = 3.0
epsilon = 1e-06

def expert_apply(operands):
    slot_rows, first_proj, second_proj = operands
    hidden = jax.nn.gelu(jnp.dot(slot_rows, first_proj, preferred_element_type=jnp.float32)).astype(jnp.bfloat16)
    return jnp.dot(hidden, second_proj, preferred_element_type=jnp.float32).astype(jnp.bfloat16)

def reference(tokens, slot_param, w_in, w_out):
    param_f = slot_param.astype(jnp.float32)
    slot_hat = (param_f * lax.rsqrt(lax.optimization_barrier(jnp.sum(param_f * param_f, axis=0, keepdims=True)) + epsilon)).astype(jnp.bfloat16)
    logits = logit_scale * jnp.dot(tokens, slot_hat, preferred_element_type=jnp.float32)
    col_peak = lax.optimization_barrier(jnp.max(logits, axis=0, keepdims=True))
    exp_terms = jnp.exp(logits - col_peak)
    col_total = lax.optimization_barrier(jnp.sum(exp_terms, axis=0))
    dispatch = exp_terms.astype(jnp.bfloat16)
    slot_sums = jnp.dot(dispatch.T, tokens, preferred_element_type=jnp.float32)
    slot_in = (slot_sums / col_total[:, None]).astype(jnp.bfloat16)
    slot_out = lax.map(expert_apply, (slot_in.reshape(EXPERTS, SLOTS, D), w_in, w_out)).reshape(SLOTS_ALL, D)
    row_peak = lax.optimization_barrier(jnp.max(logits, axis=1, keepdims=True))
    row_terms = jnp.exp(logits - row_peak)
    combine = (row_terms / lax.optimization_barrier(jnp.sum(row_terms, axis=1, keepdims=True))).astype(jnp.bfloat16)
    return jnp.dot(combine, slot_out, preferred_element_type=jnp.float32).astype(jnp.bfloat16)
```

```python
import jax
import jax.numpy as jnp
from jax import lax
from jax.sharding import Mesh, PartitionSpec as P

SLOTS = 4
logit_scale = 3.0
epsilon = 1e-06
AXES = ("x", "zl", "y", "core", "zh")
WIDE = ("x", "zl", "y", "core")
PLANE = ("x", "y")
RING = ("zl", "zh")
PAD = 128


def shift(n, k):
    return [(i, (i + k) % n) for i in range(n)]


def ring_shift(nl, nh, k):
    def place(z):
        return (z % nl) * nh + z // nl

    n = nl * nh
    return [(place(z), place((z + k) % n)) for z in range(n)]


def swap_core(a):
    return lax.ppermute(a, "core", shift(2, 1))


def to_plane(a):
    return lax.all_to_all(a, PLANE, split_axis=0, concat_axis=0, tiled=True)


def spread_plane(rows, n):
    whole = jnp.broadcast_to(rows[None], (n,) + rows.shape)
    return to_plane(whole.reshape(n * rows.shape[0], rows.shape[1]))


def pack(sums, peak, total):
    high = total.astype(jnp.bfloat16)
    low = (total - high.astype(jnp.float32)).astype(jnp.bfloat16)
    tail = jnp.concatenate(
        [peak[:, None], high[:, None], low[:, None], jnp.zeros((sums.shape[0], PAD - 3), jnp.bfloat16)], axis=1
    )
    return jnp.concatenate([sums.astype(jnp.bfloat16), tail], axis=1)


def merge(parts):
    d = parts.shape[2] - PAD
    sums = parts[:, :, :d].astype(jnp.float32)
    peaks = parts[:, :, d].astype(jnp.float32)
    totals = parts[:, :, d + 1].astype(jnp.float32) + parts[:, :, d + 2].astype(jnp.float32)
    peak = jnp.max(peaks, axis=0)
    weight = jnp.exp(peaks - peak[None])
    return (
        jnp.sum(sums * weight[:, :, None], axis=0),
        peak.astype(jnp.bfloat16),
        jnp.sum(totals * weight, axis=0),
    )


def make_body(size):
    nz, plane, ring = size["zl"], size["x"] * size["y"], size["zh"] * size["zl"]

    def body(tokens, slot_param, w_in, w_out):
        tokens_b = swap_core(tokens)
        param_f = slot_param.astype(jnp.float32)
        hat = (
            param_f * lax.rsqrt(jnp.sum(param_f * param_f, axis=0, keepdims=True) + epsilon)
        ).astype(jnp.bfloat16).T
        column = jnp.concatenate(
            [hat] + [lax.ppermute(hat, "zl", shift(nz, k)) for k in range(1, nz)], axis=0
        )
        hat_all = spread_plane(column, plane)
        nt = (((1,), (1,)), ((), ()))
        logits_a = logit_scale * lax.dot_general(tokens, hat_all, nt, preferred_element_type=jnp.float32)
        logits_b = logit_scale * lax.dot_general(tokens_b, hat_all, nt, preferred_element_type=jnp.float32)
        logits_c = swap_core(logits_b)
        peak = jnp.maximum(jnp.max(logits_a, axis=0), jnp.max(logits_b, axis=0)).astype(jnp.bfloat16)
        peak_f = peak.astype(jnp.float32)[None, :]
        exp_a = jnp.exp(logits_a - peak_f)
        exp_b = jnp.exp(logits_b - peak_f)
        total = jnp.sum(exp_a, axis=0) + jnp.sum(exp_b, axis=0)
        tn = (((0,), (0,)), ((), ()))
        sums = lax.dot_general(
            exp_a.astype(jnp.bfloat16), tokens, tn, preferred_element_type=jnp.float32
        ) + lax.dot_general(exp_b.astype(jnp.bfloat16), tokens_b, tn, preferred_element_type=jnp.float32)
        sent = pack(sums, peak, total)
        got = to_plane(sent).reshape(plane, sent.shape[0] // plane, sent.shape[1])
        sent = pack(*merge(got))
        blocks = [sent[SLOTS * k : SLOTS * (k + 1)] for k in range(nz)]
        got = jnp.stack(
            [blocks[0]] + [lax.ppermute(blocks[k % nz], RING, ring_shift(nz, 2, -k)) for k in range(1, ring)]
        )
        sums, _, total = merge(got)
        slot_in = (sums / total[:, None]).astype(jnp.bfloat16)
        hidden = jax.nn.gelu(jnp.dot(slot_in, w_in[0], preferred_element_type=jnp.float32)).astype(jnp.bfloat16)
        half = jnp.dot(hidden, w_out[0], preferred_element_type=jnp.float32).astype(jnp.bfloat16)
        halves = [half] + [lax.ppermute(half, RING, ring_shift(nz, 2, k)) for k in range(1, ring)]
        column = jnp.concatenate(
            [
                (halves[k].astype(jnp.float32) + halves[k + nz].astype(jnp.float32)).astype(jnp.bfloat16)
                for k in range(nz)
            ],
            axis=0,
        )
        out_a = spread_plane(column, plane)
        out_c = swap_core(out_a)
        row_peak = jnp.maximum(
            jnp.max(logits_a, axis=1, keepdims=True), jnp.max(logits_c, axis=1, keepdims=True)
        )
        row_a = jnp.exp(logits_a - row_peak)
        row_c = jnp.exp(logits_c - row_peak)
        row_sum = jnp.sum(row_a, axis=1, keepdims=True) + jnp.sum(row_c, axis=1, keepdims=True)
        mixed = jnp.dot(
            (row_a / row_sum).astype(jnp.bfloat16), out_a, preferred_element_type=jnp.float32
        ) + jnp.dot((row_c / row_sum).astype(jnp.bfloat16), out_c, preferred_element_type=jnp.float32)
        return mixed.astype(jnp.bfloat16)

    return body


def solution(mesh):
    fine = Mesh(mesh.devices.reshape(4, 4, 4, 2, 2), AXES)
    in_specs = (P(AXES, None), P(None, WIDE), P(WIDE, None, "zh"), P(WIDE, "zh", None))
    return jax.shard_map(
        make_body(dict(fine.shape)), mesh=fine, in_specs=in_specs, out_specs=P(AXES, None), check_vma=False
    )
```

```python
import jax
import jax.numpy as jnp
from jax import lax
from jax.experimental import pallas as pl
from jax.experimental.pallas import tpu as pltpu
from jax.sharding import Mesh, PartitionSpec as P

SLOTS = 4
logit_scale = 3.0
epsilon = 1e-06
AXES = ("x", "zl", "y", "core", "zh")
WIDE = ("x", "zl", "y", "core")
PLANE = ("x", "y")
RING = ("zl", "zh")
PAD = 128
TILE = 512
MIB = 1 << 20
NT = (((1,), (1,)), ((), ()))
VMEM = pl.BlockSpec(memory_space=pltpu.VMEM)
SMEM = pl.BlockSpec(memory_space=pltpu.SMEM)
ANY = pl.BlockSpec(memory_space=pl.ANY)
HBM = pl.BlockSpec(memory_space=pltpu.HBM)
DMA = pltpu.SemaphoreType.DMA


def shift(n, k):
    return [(i, (i + k) % n) for i in range(n)]


def swap_core(a):
    return lax.ppermute(a, "core", shift(2, 1))


def exchange(a, axes):
    return lax.all_to_all(a, axes, split_axis=0, concat_axis=0, tiled=True)


def call(kernel, out, *args, limit=8, specs=None, out_specs=None, scratch=(), flops=0):
    specs = specs or [VMEM] * len(args)
    spaces = {id(VMEM): pltpu.VMEM, id(HBM): pltpu.HBM}
    args = [
        pltpu.with_memory_space_constraint(a, spaces[id(s)]) if id(s) in spaces else a
        for a, s in zip(args, specs)
    ]
    return pl.pallas_call(
        kernel,
        out_shape=out,
        in_specs=specs,
        out_specs=out_specs or jax.tree.map(lambda _: VMEM, out),
        scratch_shapes=list(scratch),
        compiler_params=pltpu.CompilerParams(vmem_limit_bytes=limit * MIB),
        cost_estimate=pl.CostEstimate(flops=flops, bytes_accessed=1 << 20, transcendentals=0),
    )(*args)


def tail_of(peak, total):
    lane = lax.broadcasted_iota(jnp.int32, (peak.shape[0], PAD), 1)
    high = total.astype(jnp.bfloat16).astype(jnp.float32)
    low = total - high
    tail = jnp.where(lane == 0, peak, jnp.where(lane == 1, high, jnp.where(lane == 2, low, 0.0)))
    return tail.astype(jnp.bfloat16)


def fetch_kernel(*refs):
    n = len(refs) // 3
    copies = [pltpu.make_async_copy(refs[i], refs[n + i], refs[2 * n + i]) for i in range(n)]
    for c in copies:
        c.start()
    for c in copies:
        c.wait()


def hat_kernel(*refs):
    out = refs[-1]
    p = jnp.concatenate([r[...].astype(jnp.float32) for r in refs[:-1]], axis=0)
    hat = (p * lax.rsqrt(jnp.sum(p * p, axis=1, keepdims=True) + epsilon)).astype(jnp.bfloat16)
    for i in range(out.shape[0]):
        out[i] = hat


def slots_kernel(tok_a, tok_b, hat, sent, log_a, log_b):
    d = tok_a.shape[1]
    parts = []
    for tok, out in ((tok_b, log_b), (tok_a, log_a)):
        logits = logit_scale * lax.dot_general(hat[...], tok[...], NT, preferred_element_type=jnp.float32)
        out[...] = logits
        peak = jnp.max(logits, axis=1, keepdims=True).astype(jnp.bfloat16).astype(jnp.float32)
        terms = jnp.exp(logits - peak)
        parts.append((tok, terms.astype(jnp.bfloat16), peak, jnp.sum(terms, axis=1, keepdims=True)))
    peak = jnp.maximum(parts[0][2], parts[1][2])
    scale = [jnp.exp(p[2] - peak) for p in parts]
    sent[:, d:] = tail_of(peak, sum(p[3] * s for p, s in zip(parts, scale)))
    for j in range(0, d, TILE):
        cols = slice(j, j + TILE)
        sums = [jnp.dot(p[1], p[0][:, cols], preferred_element_type=jnp.float32) * s for p, s in zip(parts, scale)]
        sent[:, cols] = (sums[0] + sums[1]).astype(jnp.bfloat16)


def weights_of(tails):
    peak = tails[0][:, 0:1]
    for t in tails[1:]:
        peak = jnp.maximum(peak, t[:, 0:1])
    weights = [jnp.exp(t[:, 0:1] - peak) for t in tails]
    total = sum(w * (t[:, 1:2] + t[:, 2:3]) for w, t in zip(weights, tails))
    return peak, weights, total


def merge_kernel(place, got, after, sent):
    n, rows, wide = got.shape
    d = wide - PAD
    nz = rows // SLOTS
    copies = sent.shape[0] // nz
    peak, weights, total = weights_of([got[i, :, d:].astype(jnp.float32) for i in range(n)])

    def put(block, lo, hi):
        for k in range(nz):
            z = lax.rem(place[0] - k + nz, nz)
            for h in range(copies):
                sent[z * copies + h, :, lo:hi] = block[SLOTS * k : SLOTS * (k + 1)]

    put(tail_of(peak, total), d, wide)
    for j in range(0, d, TILE):
        acc = got[0, :, j : j + TILE].astype(jnp.float32) * weights[0]
        for i in range(1, n):
            acc += got[i, :, j : j + TILE].astype(jnp.float32) * weights[i]
        put(acc.astype(jnp.bfloat16), j, j + TILE)


def expert_kernel(got, w_in, w_out, out, in_v, out_v, sems):
    cuts = sems.shape[1]
    copies = []
    for j, (src, dst) in enumerate(((w_in, in_v), (w_out, out_v))):
        step = dst.shape[0] // cuts
        for i in range(cuts):
            rows = pl.ds(i * step, step)
            copies.append(pltpu.make_async_copy(src.at[0, rows, :], dst.at[rows, :], sems.at[j, i]))
            copies[-1].start()
    n, rows, wide = got.shape
    d = wide - PAD
    _, weights, total = weights_of([got[i, :, d:].astype(jnp.float32) for i in range(n)])
    acc = got[0, :, :d].astype(jnp.float32) * weights[0]
    for i in range(1, n):
        acc += got[i, :, :d].astype(jnp.float32) * weights[i]
    row = (acc / total).astype(jnp.bfloat16)
    for j, held in enumerate((in_v, out_v)):
        step = held.shape[0] // cuts
        acc = jnp.zeros((rows, held.shape[1]), jnp.float32)
        for i in range(cuts):
            copies[j * cuts + i].wait()
            acc += jnp.dot(
                row[:, i * step : (i + 1) * step],
                held[i * step : (i + 1) * step, :],
                preferred_element_type=jnp.float32,
            )
        row = (jax.nn.gelu(acc) if j == 0 else acc).astype(jnp.bfloat16)
    for i in range(out.shape[0]):
        out[i] = row


def column_kernel(place, got, out):
    nz = out.shape[1] // SLOTS
    copies = got.shape[0] // nz
    parts = []
    for k in range(nz):
        z = lax.rem(place[0] - k + nz, nz)
        acc = got[z * copies].astype(jnp.float32)
        for h in range(1, copies):
            acc += got[z * copies + h].astype(jnp.float32)
        parts.append(acc)
    column = jnp.concatenate(parts, axis=0).astype(jnp.bfloat16)
    for i in range(out.shape[0]):
        out[i] = column


def combine_kernel(log_a, log_c, out_a, out_c):
    peak = jnp.maximum(jnp.max(log_a[...], axis=0, keepdims=True), jnp.max(log_c[...], axis=0, keepdims=True))
    terms = [jnp.exp(r[...] - peak) for r in (log_a, log_c)]
    total = sum(jnp.sum(t, axis=0, keepdims=True) for t in terms)
    for t, out in zip(terms, (out_a, out_c)):
        out[...] = jnp.transpose(t / total).astype(jnp.bfloat16)


def mixed_kernel(w_a, w_c, out_a, out_c, mixed, held, sems):
    blocks, pieces = sems.shape
    step = w_a.shape[0] // blocks
    cut = step // pieces
    copies = []
    for i in range(blocks):
        r = pl.ds(i * step, step)
        acc = jnp.dot(w_a[r, :], out_a[...], preferred_element_type=jnp.float32)
        acc += jnp.dot(w_c[r, :], out_c[...], preferred_element_type=jnp.float32)
        held[r, :] = acc.astype(jnp.bfloat16)
        for j in range(pieces):
            c = pl.ds(i * step + j * cut, cut)
            copies.append(pltpu.make_async_copy(held.at[c, :], mixed.at[c, :], sems.at[i, j]))
            copies[-1].start()
    for c in copies:
        c.wait()


def make_body(size):
    nz, plane, ring = size["zl"], size["x"] * size["y"], size["zh"] * size["zl"]

    def body(tokens, slot_param, w_in, w_out):
        n_tok, d = tokens.shape
        rows = nz * SLOTS
        bf, f32 = jnp.bfloat16, jnp.float32
        S = jax.ShapeDtypeStruct
        place = lax.axis_index("zl").astype(jnp.int32).reshape(1)
        param = slot_param.T
        param_v, tokens_a = call(
            fetch_kernel, [pltpu.VMEM(param.shape, bf), pltpu.VMEM(tokens.shape, bf)], param, tokens,
            specs=[HBM] * 2, scratch=[DMA(())] * 2, flops=1 << 31,
        )
        blocks = [param_v] + [lax.ppermute(param, "zl", shift(nz, k)) for k in range(1, nz)]
        tokens_b = swap_core(tokens)
        own = plane * rows
        hat = exchange(call(hat_kernel, S((plane, rows, d), bf), *blocks), PLANE)
        sent, log_a, log_b = call(
            slots_kernel,
            [S((own, d + PAD), bf), S((own, n_tok), f32), S((own, n_tok), f32)],
            tokens_a, tokens_b, hat.reshape(own, d), flops=8 * own * n_tok * d,
        )
        got = exchange(sent.reshape(plane, rows, d + PAD), PLANE)
        log_c = swap_core(log_b)
        w_a, w_c = call(combine_kernel, [S((n_tok, own), bf)] * 2, log_a, log_c, flops=1 << 26)
        sent = call(
            merge_kernel, S((ring, SLOTS, d + PAD), bf), place, got, w_a, specs=[SMEM, VMEM, ANY]
        )
        got = exchange(sent, RING)
        half = call(
            expert_kernel, S((ring, SLOTS, d), bf), got, w_in, w_out, limit=14,
            specs=[VMEM, HBM, HBM],
            scratch=[pltpu.VMEM(w_in.shape[1:], bf), pltpu.VMEM(w_out.shape[1:], bf), DMA((2, 4))],
            flops=4 * SLOTS * d * w_in.shape[2]
        )
        got = exchange(half, RING)
        sent = call(column_kernel, S((plane, rows, d), bf), place, got, specs=[SMEM, VMEM])
        out_a = exchange(sent, PLANE).reshape(own, d)
        out_c = swap_core(out_a)
        mixed = call(
            mixed_kernel, S((n_tok, d), bf), w_a, w_c, out_a, out_c, out_specs=ANY, limit=8,
            scratch=[pltpu.VMEM((n_tok, d), bf), DMA((2, 4))], flops=4 * n_tok * own * d,
        )
        return mixed

    return body


def solution(mesh):
    fine = Mesh(mesh.devices.reshape(4, 4, 4, 2, 2), AXES)
    in_specs = (P(AXES, None), P(None, WIDE), P(WIDE, None, "zh"), P(WIDE, "zh", None))
    return jax.shard_map(
        make_body(dict(fine.shape)), mesh=fine, in_specs=in_specs, out_specs=P(AXES, None), check_vma=False
    )
```

```python
import jax
import jax.numpy as jnp
from jax import lax
from jax.experimental import pallas as pl
from jax.experimental.pallas import tpu as pltpu
from jax.sharding import Mesh, PartitionSpec as P

SLOTS = 4
logit_scale = 3.0
epsilon = 1e-06
AXES = ("x", "zl", "y", "core", "zh")
WIDE = ("x", "zl", "y", "core")
PLANE = ("x", "y")
RING = ("zl", "zh")
PAD = 128
TILE = 512
SUM_TILE = 1024
MIB = 1 << 20
NT = (((1,), (1,)), ((), ()))
VMEM = pl.BlockSpec(memory_space=pltpu.VMEM)
SMEM = pl.BlockSpec(memory_space=pltpu.SMEM)
ANY = pl.BlockSpec(memory_space=pl.ANY)
HBM = pl.BlockSpec(memory_space=pltpu.HBM)
DMA = pltpu.SemaphoreType.DMA


def shift(n, k):
    return [(i, (i + k) % n) for i in range(n)]


def swap_core(a):
    return lax.ppermute(a, "core", shift(2, 1))


def exchange(a, axes):
    return lax.all_to_all(a, axes, split_axis=0, concat_axis=0, tiled=True)


def call(kernel, out, *args, limit=8, specs=None, out_specs=None, scratch=(), flops=0):
    specs = specs or [VMEM] * len(args)
    spaces = {id(VMEM): pltpu.VMEM, id(HBM): pltpu.HBM}
    args = [
        pltpu.with_memory_space_constraint(a, spaces[id(s)]) if id(s) in spaces else a
        for a, s in zip(args, specs)
    ]
    return pl.pallas_call(
        kernel,
        out_shape=out,
        in_specs=specs,
        out_specs=out_specs or jax.tree.map(lambda _: VMEM, out),
        scratch_shapes=list(scratch),
        compiler_params=pltpu.CompilerParams(vmem_limit_bytes=limit * MIB),
        cost_estimate=pl.CostEstimate(flops=flops, bytes_accessed=1 << 20, transcendentals=0),
    )(*args)


def tail_of(peak, total):
    lane = lax.broadcasted_iota(jnp.int32, (peak.shape[0], PAD), 1)
    high = total.astype(jnp.bfloat16).astype(jnp.float32)
    low = total - high
    tail = jnp.where(lane == 0, peak, jnp.where(lane == 1, high, jnp.where(lane == 2, low, 0.0)))
    return tail.astype(jnp.bfloat16)


def fetch_kernel(*refs):
    n = len(refs) // 3
    copies = [pltpu.make_async_copy(refs[i], refs[n + i], refs[2 * n + i]) for i in range(n)]
    for c in copies:
        c.start()
    for c in copies:
        c.wait()


def hat_kernel(*refs):
    out = refs[-1]
    p = jnp.concatenate([r[...].astype(jnp.float32) for r in refs[:-1]], axis=0)
    hat = (p * lax.rsqrt(jnp.sum(p * p, axis=1, keepdims=True) + epsilon)).astype(jnp.bfloat16)
    for i in range(out.shape[0]):
        out[i] = hat


def pieces_kernel(whole, after, *refs):
    parts, sems = refs[:-1], refs[-1]
    step = parts[0].shape[0]
    copies = [
        pltpu.make_async_copy(whole.at[0, pl.ds(i * step, step), :], p, sems.at[i]) for i, p in enumerate(parts)
    ]
    for c in copies:
        c.start()
    for c in copies:
        c.wait()


def slots_kernel(tok_a, tok_b, hat, sent, log_a, log_b):
    d = tok_a.shape[1]
    parts = []
    for tok, out in ((tok_b, log_b), (tok_a, log_a)):
        logits = logit_scale * lax.dot_general(hat[...], tok[...], NT, preferred_element_type=jnp.float32)
        out[...] = logits
        peak = jnp.max(logits, axis=1, keepdims=True).astype(jnp.bfloat16).astype(jnp.float32)
        terms = jnp.exp(logits - peak)
        parts.append((tok, terms.astype(jnp.bfloat16), peak, jnp.sum(terms, axis=1, keepdims=True)))
    peak = jnp.maximum(parts[0][2], parts[1][2])
    scale = [jnp.exp(p[2] - peak) for p in parts]
    sent[:, d:] = tail_of(peak, sum(p[3] * s for p, s in zip(parts, scale)))
    for j in range(0, d, SUM_TILE):
        cols = slice(j, j + SUM_TILE)
        sums = [jnp.dot(p[1], p[0][:, cols], preferred_element_type=jnp.float32) * s for p, s in zip(parts, scale)]
        sent[:, cols] = (sums[0] + sums[1]).astype(jnp.bfloat16)


def weights_of(tails):
    peak = tails[0][:, 0:1]
    for t in tails[1:]:
        peak = jnp.maximum(peak, t[:, 0:1])
    weights = [jnp.exp(t[:, 0:1] - peak) for t in tails]
    total = sum(w * (t[:, 1:2] + t[:, 2:3]) for w, t in zip(weights, tails))
    return peak, weights, total


def merge_kernel(place, got, after, sent):
    n, rows, wide = got.shape
    d = wide - PAD
    nz = rows // SLOTS
    copies = sent.shape[0] // nz
    peak, weights, total = weights_of([got[i, :, d:].astype(jnp.float32) for i in range(n)])

    def put(block, lo, hi):
        for k in range(nz):
            z = lax.rem(place[0] - k + nz, nz)
            for h in range(copies):
                sent[z * copies + h, :, lo:hi] = block[SLOTS * k : SLOTS * (k + 1)]

    put(tail_of(peak, total), d, wide)
    for j in range(0, d, TILE):
        acc = got[0, :, j : j + TILE].astype(jnp.float32) * weights[0]
        for i in range(1, n):
            acc += got[i, :, j : j + TILE].astype(jnp.float32) * weights[i]
        put(acc.astype(jnp.bfloat16), j, j + TILE)


def expert_kernel(got, *refs):
    first, (w_out, out, out_v, sems) = refs[:-4], refs[-4:]
    cuts = sems.shape[0]
    step = out_v.shape[0] // cuts
    copies = []
    for i in range(cuts * 4):
        r = pl.ds(i * (step // 4), step // 4)
        copies.append(pltpu.make_async_copy(w_out.at[0, r, :], out_v.at[r, :], sems.at[i // 4, i % 4]))
        copies[-1].start()
    n, rows, wide = got.shape
    d = wide - PAD
    _, weights, total = weights_of([got[i, :, d:].astype(jnp.float32) for i in range(n)])
    acc = got[0, :, :d].astype(jnp.float32) * weights[0]
    for i in range(1, n):
        acc += got[i, :, :d].astype(jnp.float32) * weights[i]
    row = (acc / total).astype(jnp.bfloat16)
    acc = jnp.zeros((rows, w_out.shape[1]), jnp.float32)
    for i, w in enumerate(first):
        k = w.shape[0]
        acc += jnp.dot(row[:, i * k : (i + 1) * k], w[...], preferred_element_type=jnp.float32)
    row = jax.nn.gelu(acc).astype(jnp.bfloat16)
    acc = jnp.zeros((rows, d), jnp.float32)
    for i in range(cuts):
        for c in copies[4 * i : 4 * i + 4]:
            c.wait()
        r = slice(i * step, (i + 1) * step)
        acc += jnp.dot(row[:, r], out_v[r, :], preferred_element_type=jnp.float32)
    row = acc.astype(jnp.bfloat16)
    for i in range(out.shape[0]):
        out[i] = row


def column_kernel(place, got, out):
    nz = out.shape[1] // SLOTS
    copies = got.shape[0] // nz
    parts = []
    for k in range(nz):
        z = lax.rem(place[0] - k + nz, nz)
        acc = got[z * copies].astype(jnp.float32)
        for h in range(1, copies):
            acc += got[z * copies + h].astype(jnp.float32)
        parts.append(acc)
    column = jnp.concatenate(parts, axis=0).astype(jnp.bfloat16)
    for i in range(out.shape[0]):
        out[i] = column


def combine_kernel(log_a, log_c, out_a, out_c):
    peak = jnp.maximum(jnp.max(log_a[...], axis=0, keepdims=True), jnp.max(log_c[...], axis=0, keepdims=True))
    terms = [jnp.exp(r[...] - peak) for r in (log_a, log_c)]
    total = sum(jnp.sum(t, axis=0, keepdims=True) for t in terms)
    for t, out in zip(terms, (out_a, out_c)):
        out[...] = jnp.transpose(t / total).astype(jnp.bfloat16)


def first_kernel(weight, rows, acc):
    acc[...] = jnp.dot(weight[...], rows[...], preferred_element_type=jnp.float32)


def mixed_kernel(acc, weight, rows, mixed, held, sems):
    blocks = sems.shape[0]
    step = weight.shape[0] // blocks
    copies = []
    for i in range(blocks):
        r = pl.ds(i * step, step)
        total = acc[r, :] + jnp.dot(weight[r, :], rows[...], preferred_element_type=jnp.float32)
        held[r, :] = total.astype(jnp.bfloat16)
        copies.append(pltpu.make_async_copy(held.at[r, :], mixed.at[r, :], sems.at[i]))
        copies[-1].start()
    for c in copies:
        c.wait()


def make_body(size):
    nz, plane, ring = size["zl"], size["x"] * size["y"], size["zh"] * size["zl"]

    def body(tokens, slot_param, w_in, w_out):
        n_tok, d = tokens.shape
        rows = nz * SLOTS
        bf, f32 = jnp.bfloat16, jnp.float32
        S = jax.ShapeDtypeStruct
        place = lax.axis_index("zl").astype(jnp.int32).reshape(1)
        param = slot_param.T
        param_v, tokens_a = call(
            fetch_kernel, [pltpu.VMEM(param.shape, bf), pltpu.VMEM(tokens.shape, bf)], param, tokens,
            specs=[HBM] * 2, scratch=[DMA(())] * 2, flops=1 << 31,
        )
        blocks = [param_v] + [lax.ppermute(param, "zl", shift(nz, k)) for k in range(1, nz)]
        tokens_b = swap_core(tokens)
        own = plane * rows
        hat = exchange(call(hat_kernel, S((plane, rows, d), bf), *blocks), PLANE)
        sent, log_a, log_b = call(
            slots_kernel,
            [S((own, d + PAD), bf), S((own, n_tok), f32), S((own, n_tok), f32)],
            tokens_a, tokens_b, hat.reshape(own, d), flops=8 * own * n_tok * d,
        )
        got = exchange(sent.reshape(plane, rows, d + PAD), PLANE)
        log_c = swap_core(log_b)
        w_a, w_c = call(combine_kernel, [S((n_tok, own), bf)] * 2, log_a, log_c, flops=1 << 26)
        cut = (w_in.shape[1] // 4, w_in.shape[2])
        held = call(
            pieces_kernel, [pltpu.VMEM(cut, bf)] * 4, w_in, w_a, specs=[HBM, ANY], scratch=[DMA((4,))], flops=1 << 31
        )
        sent = call(
            merge_kernel, S((ring, SLOTS, d + PAD), bf), place, got, held[3], specs=[SMEM, VMEM, ANY]
        )
        got = exchange(sent, RING)
        half = call(
            expert_kernel, S((ring, SLOTS, d), bf), got, *held, w_out, limit=8,
            specs=[VMEM] * 5 + [HBM],
            scratch=[pltpu.VMEM(w_out.shape[1:], bf), DMA((4, 4))],
            flops=4 * SLOTS * d * w_in.shape[2]
        )
        got = exchange(half, RING)
        sent = call(column_kernel, S((plane, rows, d), bf), place, got, specs=[SMEM, VMEM])
        out_a = exchange(sent, PLANE).reshape(own, d)
        out_c = swap_core(out_a)
        acc = call(first_kernel, pltpu.VMEM((n_tok, d), f32), w_a, out_a, flops=2 * n_tok * own * d)
        mixed = call(
            mixed_kernel, S((n_tok, d), bf), acc, w_c, out_c, out_specs=ANY,
            scratch=[pltpu.VMEM((n_tok, d), bf), DMA((4,))], flops=2 * n_tok * own * d,
        )
        return mixed

    return body


def solution(mesh):
    fine = Mesh(mesh.devices.reshape(4, 4, 4, 2, 2), AXES)
    in_specs = (P(AXES, None), P(None, WIDE), P(WIDE, None, "zh"), P(WIDE, "zh", None))
    return jax.shard_map(
        make_body(dict(fine.shape)), mesh=fine, in_specs=in_specs, out_specs=P(AXES, None), check_vma=False
    )
```

```python
import jax
import jax.numpy as jnp
from jax import lax
from jax.experimental import pallas as pl
from jax.experimental.pallas import tpu as pltpu
from jax.sharding import Mesh, PartitionSpec as P

SLOTS = 4
logit_scale = 3.0
epsilon = 1e-06
AXES = ("x", "zl", "y", "core", "zh")
WIDE = ("x", "zl", "y", "core")
PLANE = ("x", "y")
RING = ("zl", "zh")
PAD = 128
TILE = 512
SUM_TILE = 1024
MIB = 1 << 20
NT = (((1,), (1,)), ((), ()))
VMEM = pl.BlockSpec(memory_space=pltpu.VMEM)
SMEM = pl.BlockSpec(memory_space=pltpu.SMEM)
ANY = pl.BlockSpec(memory_space=pl.ANY)
HBM = pl.BlockSpec(memory_space=pltpu.HBM)
DMA = pltpu.SemaphoreType.DMA


def shift(n, k):
    return [(i, (i + k) % n) for i in range(n)]


def swap_core(a):
    return lax.ppermute(a, "core", shift(2, 1))


def exchange(a, axes):
    return lax.all_to_all(a, axes, split_axis=0, concat_axis=0, tiled=True)


def call(kernel, out, *args, limit=8, specs=None, out_specs=None, scratch=(), flops=0):
    specs = specs or [VMEM] * len(args)
    spaces = {id(VMEM): pltpu.VMEM, id(HBM): pltpu.HBM}
    args = [
        pltpu.with_memory_space_constraint(a, spaces[id(s)]) if id(s) in spaces else a
        for a, s in zip(args, specs)
    ]
    return pl.pallas_call(
        kernel,
        out_shape=out,
        in_specs=specs,
        out_specs=out_specs or jax.tree.map(lambda _: VMEM, out),
        scratch_shapes=list(scratch),
        compiler_params=pltpu.CompilerParams(vmem_limit_bytes=limit * MIB),
        cost_estimate=pl.CostEstimate(flops=flops, bytes_accessed=1 << 20, transcendentals=0),
    )(*args)


def tail_of(peak, total):
    lane = lax.broadcasted_iota(jnp.int32, (peak.shape[0], PAD), 1)
    high = total.astype(jnp.bfloat16).astype(jnp.float32)
    low = total - high
    tail = jnp.where(lane == 0, peak, jnp.where(lane == 1, high, jnp.where(lane == 2, low, 0.0)))
    return tail.astype(jnp.bfloat16)


def fetch_kernel(*refs):
    n = len(refs) // 3
    copies = [pltpu.make_async_copy(refs[i], refs[n + i], refs[2 * n + i]) for i in range(n)]
    for c in copies:
        c.start()
    for c in copies:
        c.wait()


def hat_kernel(*refs):
    out = refs[-1]
    p = jnp.concatenate([r[...].astype(jnp.float32) for r in refs[:-1]], axis=0)
    hat = (p * lax.rsqrt(jnp.sum(p * p, axis=1, keepdims=True) + epsilon)).astype(jnp.bfloat16)
    for i in range(out.shape[0]):
        out[i] = hat


def pieces_kernel(whole, after, *refs):
    parts, sems = refs[:-1], refs[-1]
    step = parts[0].shape[0]
    copies = [
        pltpu.make_async_copy(whole.at[0, pl.ds(i * step, step), :], p, sems.at[i]) for i, p in enumerate(parts)
    ]
    for c in copies:
        c.start()
    for c in copies:
        c.wait()


def slots_kernel(tok_a, tok_b, hat, sent, log_a, log_b, held, sems):
    d = tok_a.shape[1]
    parts = []
    for tok, out in ((tok_b, log_b), (tok_a, log_a)):
        logits = logit_scale * lax.dot_general(hat[...], tok[...], NT, preferred_element_type=jnp.float32)
        out[...] = logits
        peak = jnp.max(logits, axis=1, keepdims=True).astype(jnp.bfloat16).astype(jnp.float32)
        terms = jnp.exp(logits - peak)
        parts.append((tok, terms.astype(jnp.bfloat16), peak, jnp.sum(terms, axis=1, keepdims=True)))
    peak = jnp.maximum(parts[0][2], parts[1][2])
    scale = [jnp.exp(p[2] - peak) for p in parts]
    held[:, d:] = tail_of(peak, sum(p[3] * s for p, s in zip(parts, scale)))
    copies = [pltpu.make_async_copy(held.at[:, pl.ds(d, PAD)], sent.at[:, pl.ds(d, PAD)], sems.at[0])]
    copies[0].start()
    for i in range(d // SUM_TILE):
        cols = slice(i * SUM_TILE, (i + 1) * SUM_TILE)
        sums = [jnp.dot(p[1], p[0][:, cols], preferred_element_type=jnp.float32) * s for p, s in zip(parts, scale)]
        held[:, cols] = (sums[0] + sums[1]).astype(jnp.bfloat16)
        place = pl.ds(i * SUM_TILE, SUM_TILE)
        copies.append(pltpu.make_async_copy(held.at[:, place], sent.at[:, place], sems.at[i + 1]))
        copies[-1].start()
    for c in copies:
        c.wait()


def weights_of(tails):
    peak = tails[0][:, 0:1]
    for t in tails[1:]:
        peak = jnp.maximum(peak, t[:, 0:1])
    weights = [jnp.exp(t[:, 0:1] - peak) for t in tails]
    total = sum(w * (t[:, 1:2] + t[:, 2:3]) for w, t in zip(weights, tails))
    return peak, weights, total


def merge_kernel(place, got, after, sent):
    n, rows, wide = got.shape
    d = wide - PAD
    nz = rows // SLOTS
    copies = sent.shape[0] // nz
    peak, weights, total = weights_of([got[i, :, d:].astype(jnp.float32) for i in range(n)])

    def put(block, lo, hi):
        for k in range(nz):
            z = lax.rem(place[0] - k + nz, nz)
            for h in range(copies):
                sent[z * copies + h, :, lo:hi] = block[SLOTS * k : SLOTS * (k + 1)]

    put(tail_of(peak, total), d, wide)
    for j in range(0, d, TILE):
        acc = got[0, :, j : j + TILE].astype(jnp.float32) * weights[0]
        for i in range(1, n):
            acc += got[i, :, j : j + TILE].astype(jnp.float32) * weights[i]
        put(acc.astype(jnp.bfloat16), j, j + TILE)


def expert_kernel(got, *refs):
    first, (w_out, out, out_v, sems) = refs[:-4], refs[-4:]
    cuts = sems.shape[0]
    step = out_v.shape[0] // cuts
    copies = []
    for i in range(cuts * 4):
        r = pl.ds(i * (step // 4), step // 4)
        copies.append(pltpu.make_async_copy(w_out.at[0, r, :], out_v.at[r, :], sems.at[i // 4, i % 4]))
        copies[-1].start()
    n, rows, wide = got.shape
    d = wide - PAD
    _, weights, total = weights_of([got[i, :, d:].astype(jnp.float32) for i in range(n)])
    acc = got[0, :, :d].astype(jnp.float32) * weights[0]
    for i in range(1, n):
        acc += got[i, :, :d].astype(jnp.float32) * weights[i]
    row = (acc / total).astype(jnp.bfloat16)
    acc = jnp.zeros((rows, w_out.shape[1]), jnp.float32)
    for i, w in enumerate(first):
        k = w.shape[0]
        acc += jnp.dot(row[:, i * k : (i + 1) * k], w[...], preferred_element_type=jnp.float32)
    row = jax.nn.gelu(acc).astype(jnp.bfloat16)
    acc = jnp.zeros((rows, d), jnp.float32)
    for i in range(cuts):
        for c in copies[4 * i : 4 * i + 4]:
            c.wait()
        r = slice(i * step, (i + 1) * step)
        acc += jnp.dot(row[:, r], out_v[r, :], preferred_element_type=jnp.float32)
    row = acc.astype(jnp.bfloat16)
    for i in range(out.shape[0]):
        out[i] = row


def column_kernel(place, got, out):
    nz = out.shape[1] // SLOTS
    copies = got.shape[0] // nz
    parts = []
    for k in range(nz):
        z = lax.rem(place[0] - k + nz, nz)
        acc = got[z * copies].astype(jnp.float32)
        for h in range(1, copies):
            acc += got[z * copies + h].astype(jnp.float32)
        parts.append(acc)
    column = jnp.concatenate(parts, axis=0).astype(jnp.bfloat16)
    for i in range(out.shape[0]):
        out[i] = column


def combine_kernel(log_a, log_c, out_a, out_c):
    peak = jnp.maximum(jnp.max(log_a[...], axis=0, keepdims=True), jnp.max(log_c[...], axis=0, keepdims=True))
    terms = [jnp.exp(r[...] - peak) for r in (log_a, log_c)]
    total = sum(jnp.sum(t, axis=0, keepdims=True) for t in terms)
    for t, out in zip(terms, (out_a, out_c)):
        out[...] = jnp.transpose(t / total).astype(jnp.bfloat16)


def first_kernel(weight, rows, acc):
    acc[...] = jnp.dot(weight[...], rows[...], preferred_element_type=jnp.float32)


def mixed_kernel(acc, weight, rows, mixed, held, sems):
    blocks = sems.shape[0]
    step = weight.shape[0] // blocks
    copies = []
    for i in range(blocks):
        r = pl.ds(i * step, step)
        total = acc[r, :] + jnp.dot(weight[r, :], rows[...], preferred_element_type=jnp.float32)
        held[r, :] = total.astype(jnp.bfloat16)
        copies.append(pltpu.make_async_copy(held.at[r, :], mixed.at[r, :], sems.at[i]))
        copies[-1].start()
    for c in copies:
        c.wait()


def make_body(size):
    nz, plane, ring = size["zl"], size["x"] * size["y"], size["zh"] * size["zl"]

    def body(tokens, slot_param, w_in, w_out):
        n_tok, d = tokens.shape
        rows = nz * SLOTS
        bf, f32 = jnp.bfloat16, jnp.float32
        S = jax.ShapeDtypeStruct
        place = lax.axis_index("zl").astype(jnp.int32).reshape(1)
        param = slot_param.T
        param_v, tokens_a = call(
            fetch_kernel, [pltpu.VMEM(param.shape, bf), pltpu.VMEM(tokens.shape, bf)], param, tokens,
            specs=[HBM] * 2, scratch=[DMA(())] * 2, flops=1 << 31,
        )
        blocks = [param_v] + [lax.ppermute(param, "zl", shift(nz, k)) for k in range(1, nz)]
        tokens_b = swap_core(tokens)
        own = plane * rows
        hat = exchange(call(hat_kernel, S((plane, rows, d), bf), *blocks), PLANE)
        sent, log_a, log_b = call(
            slots_kernel,
            [S((own, d + PAD), bf), S((own, n_tok), f32), S((own, n_tok), f32)],
            tokens_a, tokens_b, hat.reshape(own, d), flops=8 * own * n_tok * d,
            out_specs=[ANY, VMEM, VMEM], scratch=[pltpu.VMEM((own, d + PAD), bf), DMA((d // SUM_TILE + 1,))],
        )
        got = exchange(sent.reshape(plane, rows, d + PAD), PLANE)
        log_c = swap_core(log_b)
        w_a, w_c = call(combine_kernel, [S((n_tok, own), bf)] * 2, log_a, log_c, flops=1 << 26)
        cut = (w_in.shape[1] // 4, w_in.shape[2])
        held = call(
            pieces_kernel, [pltpu.VMEM(cut, bf)] * 4, w_in, w_a, specs=[HBM, ANY], scratch=[DMA((4,))], flops=1 << 31
        )
        sent = call(
            merge_kernel, S((ring, SLOTS, d + PAD), bf), place, got, held[3], specs=[SMEM, VMEM, ANY]
        )
        got = exchange(sent, RING)
        half = call(
            expert_kernel, S((ring, SLOTS, d), bf), got, *held, w_out, limit=8,
            specs=[VMEM] * 5 + [HBM],
            scratch=[pltpu.VMEM(w_out.shape[1:], bf), DMA((4, 4))],
            flops=4 * SLOTS * d * w_in.shape[2]
        )
        got = exchange(half, RING)
        sent = call(column_kernel, S((plane, rows, d), bf), place, got, specs=[SMEM, VMEM])
        out_a = exchange(sent, PLANE).reshape(own, d)
        out_c = swap_core(out_a)
        acc = call(first_kernel, pltpu.VMEM((n_tok, d), f32), w_a, out_a, flops=2 * n_tok * own * d)
        mixed = call(
            mixed_kernel, S((n_tok, d), bf), acc, w_c, out_c, out_specs=ANY,
            scratch=[pltpu.VMEM((n_tok, d), bf), DMA((4,))], flops=2 * n_tok * own * d,
        )
        return mixed

    return body


def solution(mesh):
    fine = Mesh(mesh.devices.reshape(4, 4, 4, 2, 2), AXES)
    in_specs = (P(AXES, None), P(None, WIDE), P(WIDE, None, "zh"), P(WIDE, "zh", None))
    return jax.shard_map(
        make_body(dict(fine.shape)), mesh=fine, in_specs=in_specs, out_specs=P(AXES, None), check_vma=False
    )
```
